32 devices in a mesh: groups: 2 (over y), ctx: 16 (over z, x, core).
Axes of the slice: x: 2, y: 2, z: 4, core: 2. Of those that a mesh axis runs over, the one named last changes fastest.
Arguments:
- q_nope: bfloat16 [4096, 8192], P(('groups', 'ctx')), parts along dimension 0, may hold values from -6 to 6
- q_rope: bfloat16 [4096, 4096], P(('groups', 'ctx')), parts along dimension 0, may hold values from -240 to 240
- latent: bfloat16 [4096, 576], P(('groups', 'ctx')), parts along dimension 0, may hold values from -4 to 4
- w_uk: bfloat16 [512, 8192], P('ctx'), may hold values from -0.5 to 0.5
- w_uv: bfloat16 [512, 8192], P('ctx'), may hold values from -0.25 to 0.25
- doc_lengths: int32 [16], P('groups'), parts along dimension 0, may hold values from 1 to 512, 2048 in all
Outputs:
- attended: bfloat16 [4096, 8192], P(('groups', 'ctx')), parts along dimension 0
The draws below stay inside these ranges and needn't reach their ends.
There are 2 independent parts, one for each index of `groups`. The reference program is written for one: setup_inputs(seed, part) draws one part's arguments, and reference() takes and returns one part's arrays. A program takes and returns all parts, laid end to end along the dimension named above; an argument that names none is the same for every part. Nothing has to cross between parts.
Inputs may be any that keep to these rules, and one draw needn't show every extreme that they name: `doc_lengths`: the documents fill the context exactly, and one of them has 512 tokens.
All inputs are finite; a program needn't handle non-finite values.
Results may differ from the reference program's by a relative error of at most 0.0065.
Values may be sent and summed in bfloat16 or wider, within the bound.
A program may use at most 128 MiB of HBM per device.

```python
import math
import jax
import jax.numpy as jnp
import numpy as np
from jax import lax

HEADS = 64
DN = 128
DV = 128
DR = 64
LAT = 512
MAXDOC = 512
TOKENS = 2048
DOCS = 8


def rope_rows(key):
    return jnp.clip(jax.random.normal(key, (TOKENS, DR), jnp.float32), -4.0, 4.0)


def draw_latent(key, part):
    rope = rope_rows(key)
    key = jax.random.fold_in(key, 11)
    compressed = jnp.clip(jax.random.normal(key, (TOKENS, LAT), jnp.float32), -4.0, 4.0)
    return jnp.concatenate([compressed, rope], axis=1).astype(jnp.bfloat16)


def draw_q_rope(key, part):
    key = jax.random.fold_in(key, 12)
    base = jnp.clip(jax.random.normal(key, (TOKENS, HEADS, DR), jnp.float32), -4.0, 4.0)
    return base.reshape(TOKENS, HEADS * DR).astype(jnp.bfloat16)


def level_of(key, extent, pieces, least, high):
    factor_of = 1.0
    for axis_at, parts in pieces:
        heights = jax.random.uniform(jax.random.fold_in(jax.random.fold_in(key, 6), axis_at), (parts,), jnp.float32, least / len(pieces), high / len(pieces))
        factor_of = factor_of * jnp.repeat(jnp.exp(heights), extent[axis_at] // parts).reshape((-1,) + (1,) * (len(extent) - 1 - axis_at))
    return factor_of


def split_up(amount, total, bound, skew):
    weights = [(1 << 20) // math.isqrt(rank ** skew) + 1 for rank in range(2, amount + 1)]
    surplus, given = total - bound - (amount - 1), [1] * (amount - 1)
    while surplus > 0:
        candidates = [i for i in range(amount - 1) if given[i] < bound]
        pool, left = sum([weights[i] for i in candidates]), surplus
        for i in candidates:
            addition = min(bound - given[i], max(1, left * weights[i] // pool), surplus)
            given[i] = given[i] + addition
            surplus = surplus - addition
    return np.array([bound] + given)


def ragged(stream_key, amount, total, limit, skew):
    if amount == 2:
        one = jax.random.randint(stream_key, (), max(1, total - limit), min(limit, total - 1) + 1)
        return jnp.stack([one, total - one])
    sizes = jnp.asarray(split_up(amount, total, limit, skew), jnp.int32)
    couples = (amount - 1) // 2
    source_of, sink = sizes[1:1 + 2 * couples:2], sizes[2:2 + 2 * couples:2]
    room = jnp.minimum(source_of - 1, limit - sink)
    moved = jax.random.randint(jax.random.fold_in(stream_key, 1), (couples,), 0, 1 << 20) % (room + 1)
    sizes = sizes.at[1:1 + 2 * couples:2].set(source_of - moved).at[2:2 + 2 * couples:2].set(sink + moved)
    return sizes[jax.random.permutation(jax.random.fold_in(stream_key, 2), amount)]


def normal_values(key, extent, scale, reach, split=(), kind=jnp.bfloat16):
    array = scale * jax.random.normal(key, extent, jnp.float32)
    if split:
        array = array * level_of(key, extent, split, -0.22, 0.18)
    return jnp.clip(array, -reach, reach).astype(kind)


def setup_inputs(seed: int = 0, part: int = 0) -> dict:
    streams_of = jax.random.split(jax.random.key(seed), 7)
    part_splits = jax.random.split(jax.random.fold_in(streams_of[6], part), 7)
    q_nope = normal_values(part_splits[0], (TOKENS, HEADS * DN), 1.0, 6.0, ((0, 16),))
    q_rope = draw_q_rope(jax.random.fold_in(jax.random.fold_in(streams_of[6], part), 71), part)
    latent = draw_latent(jax.random.fold_in(jax.random.fold_in(streams_of[6], part), 71), part)
    w_uk = normal_values(streams_of[3], (LAT, HEADS * DN), DN ** -0.5, 0.5, ((0, 16),))
    w_uv = normal_values(streams_of[4], (LAT, HEADS * DV), LAT ** -0.5, 0.25, ((0, 16),))
    doc_lengths = ragged(part_splits[5], DOCS, TOKENS, MAXDOC, 2).astype(jnp.int32)
    return {"q_nope": q_nope, "q_rope": q_rope, "latent": latent, "w_uk": w_uk, "w_uv": w_uv, "doc_lengths": doc_lengths}


def doc_index(doc_lengths, positions):
    starts = jnp.cumsum(doc_lengths) - doc_lengths
    return lax.optimization_barrier(jnp.sum((starts[None, :] <= positions[:, None]).astype(jnp.int32), axis=1)) - 1

def reference(q_nope, q_rope, latent, w_uk, w_uv, doc_lengths):
    block = min(512, TOKENS // 2)
    window = block + MAXDOC
    scale = 1.0 / math.sqrt(DN + DR)
    all_doc = doc_index(doc_lengths, jnp.arange(TOKENS, dtype=jnp.int32))
    w_key = w_uk.reshape(LAT, HEADS, DN).astype(jnp.float32)
    w_value = w_uv.reshape(LAT, HEADS, DV).astype(jnp.float32)

    def one_block(start):
        start = start.astype(jnp.int32)
        queries = lax.dynamic_slice_in_dim(q_nope, start, block, 0).reshape(block, HEADS, DN).astype(jnp.float32)
        absorbed = jnp.einsum('thd,jhd->thj', queries, w_key).astype(jnp.bfloat16)
        rope_q = lax.dynamic_slice_in_dim(q_rope, start, block, 0).reshape(block, HEADS, DR).astype(jnp.float32)
        key_start = jnp.clip(start - MAXDOC, 0, TOKENS - window).astype(jnp.int32)
        keys = lax.dynamic_slice_in_dim(latent, key_start, window, 0).astype(jnp.float32)
        scores = jnp.einsum('thj,kj->thk', absorbed.astype(jnp.float32), keys[:, :LAT])
        scores = (scores + jnp.einsum('thr,kr->thk', rope_q, keys[:, LAT:])) * scale
        q_pos = start + jnp.arange(block, dtype=jnp.int32)
        k_pos = key_start + jnp.arange(window, dtype=jnp.int32)
        q_doc = lax.dynamic_slice_in_dim(all_doc, start, block, 0)
        k_doc = lax.dynamic_slice_in_dim(all_doc, key_start, window, 0)
        allowed = (q_doc[:, None] == k_doc[None, :]) & (k_pos[None, :] <= q_pos[:, None])
        allowed = allowed[:, None, :]
        top = lax.optimization_barrier(jnp.max(jnp.where(allowed, scores, jnp.float32(-1e+30)), axis=-1))
        weights = jnp.where(allowed, jnp.exp(scores - top[..., None]), jnp.float32(0.0))
        total = lax.optimization_barrier(jnp.sum(weights, axis=-1))
        weights_b = weights.astype(jnp.bfloat16).astype(jnp.float32)
        summed = jnp.einsum('thk,kj->thj', weights_b, keys[:, :LAT])
        mixed = (summed / total[..., None]).astype(jnp.bfloat16).astype(jnp.float32)
        result = jnp.einsum('thj,jhd->thd', mixed, w_value)
        return result.reshape(block, HEADS * DV).astype(jnp.bfloat16)
    block_starts = jnp.arange(0, TOKENS, block, dtype=jnp.int32)
    outputs = lax.map(one_block, block_starts)
    return outputs.reshape(TOKENS, HEADS * DV)
```

```python
import math

import jax
import jax.numpy as jnp
from jax import lax
from jax.experimental import pallas as pl
from jax.experimental.pallas import tpu as pltpu
from jax.sharding import PartitionSpec as P

HEADS = 64
DN = 128
DV = 128
DR = 64
LAT = 512
SPAN = 4
MESH = pl.DeviceIdType.MESH
Z_AHEAD = 4
X_AHEAD = 2


def from_behind(block, axis, distance):
    devices = range(lax.axis_size(axis))
    route = [(i - distance, i) for i in devices if i - distance in devices]
    return lax.ppermute(block, axis, route)


def doc_index(starts, positions):
    return jnp.sum((starts[None, :] <= positions[:, None]).astype(jnp.int32), axis=1) - 1


def allowed_pairs(starts, key_start, key_count, q_pos, q_doc):
    k_pos = key_start + jnp.arange(key_count, dtype=jnp.int32)
    k_doc = doc_index(starts, k_pos)
    return (q_doc[:, None] == k_doc[None, :]) & (k_pos[None, :] <= q_pos[:, None])


def attend(state, keys, allowed, absorbed, rope_q, scale):
    top, total, summed = state
    scores = jnp.einsum("thj,kj->thk", absorbed, keys[:, :LAT], preferred_element_type=jnp.float32)
    scores = scores + jnp.einsum(
        "thr,kr->thk", rope_q, keys[:, LAT:], preferred_element_type=jnp.float32
    )
    scores = scores * scale
    mask = allowed[:, None, :]
    fresh = jnp.maximum(top, jnp.max(jnp.where(mask, scores, jnp.float32(-1e30)), axis=-1))
    weights = jnp.where(mask, jnp.exp(scores - fresh[..., None]), jnp.float32(0.0))
    factor = jnp.exp(top - fresh)
    total = total * factor + jnp.sum(weights, axis=-1)
    summed = summed * factor[..., None] + jnp.einsum(
        "thk,kj->thj",
        weights.astype(jnp.bfloat16),
        keys[:, :LAT],
        preferred_element_type=jnp.float32,
    )
    return (fresh, total, summed)


def shards(q_nope, q_rope, latent, w_uk, w_uv, doc_lengths):
    rows_here = q_nope.shape[0]
    scale = 1.0 / math.sqrt(DN + DR)
    place = lax.axis_index("ctx")
    queries = q_nope.reshape(rows_here, HEADS, DN)
    rope_q = q_rope.reshape(rows_here, HEADS, DR)
    piece = lax.all_gather(w_uk, "ctx", axis=0, tiled=True)
    weights = piece.reshape(piece.shape[0], HEADS, DN)
    absorbed = jnp.einsum(
        "thd,jhd->thj", queries, weights, preferred_element_type=jnp.float32
    ).astype(jnp.bfloat16)
    starts = jnp.cumsum(doc_lengths) - doc_lengths
    q_pos = place * rows_here + jnp.arange(rows_here, dtype=jnp.int32)
    q_doc = doc_index(starts, q_pos)
    state = (
        jnp.full((rows_here, HEADS), -1e30, jnp.float32),
        jnp.zeros((rows_here, HEADS), jnp.float32),
        jnp.zeros((rows_here, HEADS, LAT), jnp.float32),
    )

    def take_block(carry, keys, key_start):
        allowed = allowed_pairs(starts, key_start, keys.shape[0], q_pos, q_doc)
        return lax.cond(
            jnp.any(allowed),
            lambda value: attend(value, keys, allowed, absorbed, rope_q, scale),
            lambda value: value,
            carry,
        )

    state = take_block(state, latent, place * rows_here)
    moving = latent
    for back in range(1, SPAN + 1):
        moving = from_behind(moving, "ctx", 1)
        state = take_block(state, moving, (place - back) * rows_here)
    top, total, summed = state
    mixed = (summed / total[..., None]).astype(jnp.bfloat16)
    piece = lax.all_gather(w_uv, "ctx", axis=0, tiled=True)
    rows = piece.shape[0]
    weights = piece.reshape(rows, HEADS, DV)
    term = jnp.einsum("thj,jhd->thd", mixed, weights, preferred_element_type=jnp.float32)
    result = term.reshape(rows_here, HEADS * DV)
    return result.astype(jnp.bfloat16)


HG = 4
SPREAD = 5


def window_kernel(
    qn_hbm, qr_hbm, lat_hbm, uk_hbm, uv_hbm, lens, out,
    qn, qr, win, keys, bias, lhs, wts,
    local_sem, lat_send, lat_recv, z_send, z_recv, x_send, x_recv, y_send, y_recv, c_send, c_recv,
):
    rows = qn_hbm.shape[0]
    steps = HEADS // HG
    cols = HG * DN
    n = lax.axis_size("ctx")
    group = lax.axis_index("groups")
    place = lax.axis_index("ctx")
    z = place // 4
    x = (place // 2) % 2
    c = place % 2
    half = uk_hbm.shape[0] // 2
    mine = pl.ds(pl.multiple_of(group * half, half), half)
    theirs = pl.ds(pl.multiple_of((1 - group) * half, half), half)
    weights = (uk_hbm, uv_hbm)

    def at_ctx(i):
        return (group, i)

    x_peer = at_ctx((z * 2 + (1 - x)) * 2 + c)
    c_peer = at_ctx((z * 2 + x) * 2 + (1 - c))
    y_peer = (1 - group, place)

    def plane(d):
        return lax.rem(z + d, 4)

    def z_peer(d):
        return at_ctx((plane(d) * 2 + x) * 2 + c)

    def chunk(k):
        return pl.ds(pl.multiple_of(k * cols, cols), cols)

    def remote(src, dst, send, recv, peer):
        return pltpu.make_async_remote_copy(
            src_ref=src, dst_ref=dst, send_sem=send, recv_sem=recv, device_id=peer, device_id_type=MESH
        )

    locals_ = [
        pltpu.make_async_copy(lat_hbm, win.at[SPREAD - 1], local_sem.at[0]),
        pltpu.make_async_copy(qn_hbm, qn, local_sem.at[1]),
        pltpu.make_async_copy(qr_hbm, qr, local_sem.at[2]),
    ]

    def own(k, m):
        return pltpu.make_async_copy(
            weights[m].at[:, chunk(k)], wts.at[k, m, z, x, c], local_sem.at[3 + m * steps + k]
        )

    barrier = pltpu.get_barrier_semaphore()
    offsets = (1, 2, 3, 4, 8, n - 4, n - 3, n - 2, n - 1)
    for d in offsets:
        pl.semaphore_signal(barrier, inc=1, device_id=at_ctx(lax.rem(place + d, n)), device_id_type=MESH)
    pl.semaphore_signal(barrier, inc=1, device_id=y_peer, device_id_type=MESH)
    for copy in locals_:
        copy.start()

    @pl.loop(0, steps)
    def _(k):
        own(k, 0).start()
        own(k, 1).start()

    pl.semaphore_wait(barrier, len(offsets) + 1)

    def z_copy(k, d, m):
        return remote(
            weights[m].at[mine, chunk(k)], wts.at[k, m, z, x, c, mine], z_send.at[k, d - 1, m], z_recv.at[k, d - 1, m], z_peer(d)
        )

    def z_arrival(k, d, m):
        slot = wts.at[k, m, plane(4 - d), x, c, mine]
        return remote(slot, slot, z_send.at[k, d - 1, m], z_recv.at[k, d - 1, m], z_peer(d))

    def x_own(k, m):
        return remote(
            weights[m].at[:, chunk(k)], wts.at[k, m, z, x, c], x_send.at[k, 3 + m], x_recv.at[k, 3 + m], x_peer
        )

    def x_own_arrival(k, m):
        slot = wts.at[k, m, z, 1 - x, c]
        return remote(slot, slot, x_send.at[k, 3 + m], x_recv.at[k, 3 + m], x_peer)

    def x_copy(k, d):
        slot = wts.at[k, :, plane(d), x, c, mine]
        return remote(slot, slot, x_send.at[k, d - 1], x_recv.at[k, d - 1], x_peer)

    def x_arrival(k, d):
        slot = wts.at[k, :, plane(d), 1 - x, c, mine]
        return remote(slot, slot, x_send.at[k, d - 1], x_recv.at[k, d - 1], x_peer)

    def y_copy(k, d):
        slot = wts.at[k, :, plane(d), :, c, mine]
        return remote(slot, slot, y_send.at[k, d - 1], y_recv.at[k, d - 1], y_peer)

    def y_arrival(k, d):
        slot = wts.at[k, :, plane(d), :, c, theirs]
        return remote(slot, slot, y_send.at[k, d - 1], y_recv.at[k, d - 1], y_peer)

    def c_copy(k):
        slot = wts.at[k, :, :, :, c]
        return remote(slot, slot, c_send.at[k], c_recv.at[k], c_peer)

    def c_arrival(k):
        slot = wts.at[k, :, :, :, 1 - c]
        return remote(slot, slot, c_send.at[k], c_recv.at[k], c_peer)

    def lat_copy(d):
        return remote(
            lat_hbm, win.at[SPREAD - 1 - d], lat_send.at[d - 1], lat_recv.at[d - 1], at_ctx(lax.rem(place + d, n))
        )

    def start_z(k):
        for d in (1, 3, 2):
            for m in range(2):
                z_copy(k, d, m).start()

    def start_x_own(k):
        for m in range(2):
            x_own(k, m).start()

    @pl.loop(0, X_AHEAD)
    def _(k):
        start_x_own(k)

    @pl.loop(0, Z_AHEAD // 2)
    def _(k):
        start_z(k)

    for d in range(1, SPREAD):
        lat_copy(d).start()

    @pl.loop(Z_AHEAD // 2, Z_AHEAD)
    def _(k):
        start_z(k)

    q_pos = place * rows + lax.broadcasted_iota(jnp.int32, (rows, SPREAD * rows), 0)
    k_pos = (place - (SPREAD - 1)) * rows + lax.broadcasted_iota(jnp.int32, (rows, SPREAD * rows), 1)
    low = jnp.zeros_like(q_pos)
    start = jnp.int32(0)
    for e in range(lens.shape[0]):
        low = jnp.where(q_pos >= start, start, low)
        start = start + lens[e]
    bias[...] = jnp.where((k_pos <= q_pos) & (k_pos >= low), jnp.float32(0.0), jnp.float32(-1e30))

    for copy in locals_:
        copy.wait()

    @pl.loop(0, steps)
    def _(k):
        own(k, 0).wait()
        own(k, 1).wait()

    scale = math.log2(math.e) / math.sqrt(DN + DR)
    nt = (((1,), (1,)), ((), ()))
    lane = lax.broadcasted_iota(jnp.int32, (1, 2 * DR), 1)
    sides = [
        (lane < DR).astype(jnp.float32).astype(jnp.bfloat16),
        (lane >= DR).astype(jnp.float32).astype(jnp.bfloat16),
    ]

    def attend_chunk(k):
        for pair in range(HG // 2):
            both = qr[:, pl.ds(pl.multiple_of((k * (HG // 2) + pair) * 2 * DR, 2 * DR), 2 * DR)]
            for side in range(2):
                i = pair * 2 + side
                q = qn[:, pl.ds(pl.multiple_of(k * cols + i * DN, DN), DN)]
                w = wts[k, 0, :, :, :, :, i * DN : (i + 1) * DN].reshape(LAT, DN)
                a = lax.dot_general(q, w, nt, preferred_element_type=jnp.float32)
                lhs[i * rows : (i + 1) * rows, :LAT] = a.astype(jnp.bfloat16)
                lhs[i * rows : (i + 1) * rows, LAT:] = both * sides[side]
        for pair in range(HG // 2):
            part = lhs[pair * 2 * rows : (pair + 1) * 2 * rows, :]
            s = lax.dot_general(part, keys[...], nt, preferred_element_type=jnp.float32)
            s = s.reshape(2, rows, SPREAD * rows) * scale + bias[...][None]
            s = s.reshape(2 * rows, SPREAD * rows)
            p = jnp.exp2(s - jnp.max(s, axis=-1, keepdims=True))
            total = jnp.sum(p, axis=-1, keepdims=True)
            mixed = jnp.dot(p.astype(jnp.bfloat16), keys[:, :LAT], preferred_element_type=jnp.float32)
            mixed = (mixed * (1.0 / total)).astype(jnp.bfloat16)
            for side in range(2):
                i = pair * 2 + side
                w = wts[k, 1, :, :, :, :, i * DV : (i + 1) * DV].reshape(LAT, DV)
                o = jnp.dot(mixed[side * rows : (side + 1) * rows], w, preferred_element_type=jnp.float32)
                out[:, pl.ds(pl.multiple_of(k * cols + i * DV, DV), DV)] = o.astype(out.dtype)

    @pl.loop(0, steps + 3)
    def _(s):
        @pl.when(s < steps)
        def _():
            for d in range(1, 4):
                for m in range(2):
                    z_arrival(s, d, m).wait_recv()
            for d in range(1, 4):
                x_copy(s, d).start()

        @pl.when(s + X_AHEAD < steps)
        def _():
            start_x_own(s + X_AHEAD)

        @pl.when(s + Z_AHEAD < steps)
        def _():
            start_z(s + Z_AHEAD)

        @pl.when((s >= 1) & (s <= steps))
        def _():
            k = s - 1
            for m in range(2):
                x_own_arrival(k, m).wait_recv()
            for d in range(1, 4):
                x_arrival(k, d).wait_recv()
            for d in range(1, 4):
                y_copy(k, d).start()

        @pl.when((s >= 2) & (s <= steps + 1))
        def _():
            k = s - 2
            for d in range(1, 4):
                y_arrival(k, d).wait_recv()
            c_copy(k).start()

        @pl.when(s == 2)
        def _():
            for d in range(1, SPREAD):
                lat_copy(d).wait_recv()
            for b in range(SPREAD):
                block = win[b]
                keys[b * rows : (b + 1) * rows, : LAT + DR] = block
                keys[b * rows : (b + 1) * rows, LAT + DR :] = block[:, LAT:]

        @pl.when(s >= 3)
        def _():
            k = s - 3
            c_arrival(k).wait_recv()
            attend_chunk(k)

    for d in range(1, SPREAD):
        lat_copy(d).wait_send()

    @pl.loop(0, steps)
    def _(k):
        for d in range(1, 4):
            for m in range(2):
                z_copy(k, d, m).wait_send()
            x_copy(k, d).wait_send()
            y_copy(k, d).wait_send()
        for m in range(2):
            x_own(k, m).wait_send()
        c_copy(k).wait_send()


def kernel_shards(q_nope, q_rope, latent, w_uk, w_uv, doc_lengths):
    rows = q_nope.shape[0]
    steps = HEADS // HG
    window = SPREAD * rows
    anywhere = pl.BlockSpec(memory_space=pl.ANY)
    dma = pltpu.SemaphoreType.DMA
    return pl.pallas_call(
        window_kernel,
        out_shape=jax.ShapeDtypeStruct((rows, HEADS * DV), jnp.bfloat16),
        in_specs=[anywhere] * 5 + [pl.BlockSpec(memory_space=pltpu.SMEM)],
        out_specs=pl.BlockSpec(memory_space=pltpu.VMEM),
        scratch_shapes=[
            pltpu.VMEM(q_nope.shape, jnp.bfloat16),
            pltpu.VMEM(q_rope.shape, jnp.bfloat16),
            pltpu.VMEM((SPREAD, rows, LAT + DR), jnp.bfloat16),
            pltpu.VMEM((window, LAT + 2 * DR), jnp.bfloat16),
            pltpu.VMEM((rows, window), jnp.float32),
            pltpu.VMEM((HG * rows, LAT + 2 * DR), jnp.bfloat16),
            pltpu.VMEM((steps, 2, 4, 2, 2, w_uk.shape[0], HG * DN), jnp.bfloat16),
            dma((3 + 2 * steps,)),
            dma((SPREAD - 1,)),
            dma((SPREAD - 1,)),
            dma((steps, 3, 2)),
            dma((steps, 3, 2)),
            dma((steps, 5)),
            dma((steps, 5)),
            dma((steps, 3)),
            dma((steps, 3)),
            dma((steps,)),
            dma((steps,)),
        ],
        compiler_params=pltpu.CompilerParams(
            collective_id=0, has_side_effects=True, vmem_limit_bytes=48 * 1024 * 1024
        ),
    )(q_nope, q_rope, latent, w_uk, w_uv, doc_lengths)


def solution(mesh):
    placed = (
        P(("groups", "ctx"), None),
        P(("groups", "ctx"), None),
        P(("groups", "ctx"), None),
        P("ctx", None),
        P("ctx", None),
        P("groups"),
    )
    small = mesh.shape["ctx"] == 16 and mesh.shape["groups"] == 2
    return jax.shard_map(
        kernel_shards if small else shards,
        mesh=mesh,
        in_specs=placed,
        out_specs=P(("groups", "ctx"), None),
        check_vma=False,
    )
```

```python
import math

import jax
import jax.numpy as jnp
from jax import lax
from jax.experimental import pallas as pl
from jax.experimental.pallas import tpu as pltpu
from jax.sharding import PartitionSpec as P

HEADS = 64
DN = 128
DV = 128
DR = 64
LAT = 512
SPAN = 4
MESH = pl.DeviceIdType.MESH
Z_AHEAD = 2
X_AHEAD = 1


def from_behind(block, axis, distance):
    devices = range(lax.axis_size(axis))
    route = [(i - distance, i) for i in devices if i - distance in devices]
    return lax.ppermute(block, axis, route)


def doc_index(starts, positions):
    return jnp.sum((starts[None, :] <= positions[:, None]).astype(jnp.int32), axis=1) - 1


def allowed_pairs(starts, key_start, key_count, q_pos, q_doc):
    k_pos = key_start + jnp.arange(key_count, dtype=jnp.int32)
    k_doc = doc_index(starts, k_pos)
    return (q_doc[:, None] == k_doc[None, :]) & (k_pos[None, :] <= q_pos[:, None])


def attend(state, keys, allowed, absorbed, rope_q, scale):
    top, total, summed = state
    scores = jnp.einsum("thj,kj->thk", absorbed, keys[:, :LAT], preferred_element_type=jnp.float32)
    scores = scores + jnp.einsum(
        "thr,kr->thk", rope_q, keys[:, LAT:], preferred_element_type=jnp.float32
    )
    scores = scores * scale
    mask = allowed[:, None, :]
    fresh = jnp.maximum(top, jnp.max(jnp.where(mask, scores, jnp.float32(-1e30)), axis=-1))
    weights = jnp.where(mask, jnp.exp(scores - fresh[..., None]), jnp.float32(0.0))
    factor = jnp.exp(top - fresh)
    total = total * factor + jnp.sum(weights, axis=-1)
    summed = summed * factor[..., None] + jnp.einsum(
        "thk,kj->thj",
        weights.astype(jnp.bfloat16),
        keys[:, :LAT],
        preferred_element_type=jnp.float32,
    )
    return (fresh, total, summed)


def shards(q_nope, q_rope, latent, w_uk, w_uv, doc_lengths):
    rows_here = q_nope.shape[0]
    scale = 1.0 / math.sqrt(DN + DR)
    place = lax.axis_index("ctx")
    queries = q_nope.reshape(rows_here, HEADS, DN)
    rope_q = q_rope.reshape(rows_here, HEADS, DR)
    piece = lax.all_gather(w_uk, "ctx", axis=0, tiled=True)
    weights = piece.reshape(piece.shape[0], HEADS, DN)
    absorbed = jnp.einsum(
        "thd,jhd->thj", queries, weights, preferred_element_type=jnp.float32
    ).astype(jnp.bfloat16)
    starts = jnp.cumsum(doc_lengths) - doc_lengths
    q_pos = place * rows_here + jnp.arange(rows_here, dtype=jnp.int32)
    q_doc = doc_index(starts, q_pos)
    state = (
        jnp.full((rows_here, HEADS), -1e30, jnp.float32),
        jnp.zeros((rows_here, HEADS), jnp.float32),
        jnp.zeros((rows_here, HEADS, LAT), jnp.float32),
    )

    def take_block(carry, keys, key_start):
        allowed = allowed_pairs(starts, key_start, keys.shape[0], q_pos, q_doc)
        return lax.cond(
            jnp.any(allowed),
            lambda value: attend(value, keys, allowed, absorbed, rope_q, scale),
            lambda value: value,
            carry,
        )

    state = take_block(state, latent, place * rows_here)
    moving = latent
    for back in range(1, SPAN + 1):
        moving = from_behind(moving, "ctx", 1)
        state = take_block(state, moving, (place - back) * rows_here)
    top, total, summed = state
    mixed = (summed / total[..., None]).astype(jnp.bfloat16)
    piece = lax.all_gather(w_uv, "ctx", axis=0, tiled=True)
    rows = piece.shape[0]
    weights = piece.reshape(rows, HEADS, DV)
    term = jnp.einsum("thj,jhd->thd", mixed, weights, preferred_element_type=jnp.float32)
    result = term.reshape(rows_here, HEADS * DV)
    return result.astype(jnp.bfloat16)


HG = 4
SPREAD = 5


def window_kernel(
    qn_hbm, qr_hbm, lat_hbm, uk_hbm, uv_hbm, lens, out,
    qn, qr, win, keys, bias, lhs, wts,
    local_sem, lat_send, lat_recv, z_send, z_recv, x_send, x_recv, y_send, y_recv, c_send, c_recv,
):
    rows = qn_hbm.shape[0]
    steps = HEADS // HG
    cols = HG * DN
    n = lax.axis_size("ctx")
    group = lax.axis_index("groups")
    place = lax.axis_index("ctx")
    z = place // 4
    x = (place // 2) % 2
    c = place % 2
    half = uk_hbm.shape[0] // 2
    mine = pl.ds(pl.multiple_of(group * half, half), half)
    theirs = pl.ds(pl.multiple_of((1 - group) * half, half), half)
    weights = (uk_hbm, uv_hbm)

    def at_ctx(i):
        return (group, i)

    x_peer = at_ctx((z * 2 + (1 - x)) * 2 + c)
    c_peer = at_ctx((z * 2 + x) * 2 + (1 - c))
    y_peer = (1 - group, place)

    def plane(d):
        return lax.rem(z + d, 4)

    def z_peer(d):
        return at_ctx((plane(d) * 2 + x) * 2 + c)

    def chunk(k):
        return pl.ds(pl.multiple_of(k * cols, cols), cols)

    def remote(src, dst, send, recv, peer):
        return pltpu.make_async_remote_copy(
            src_ref=src, dst_ref=dst, send_sem=send, recv_sem=recv, device_id=peer, device_id_type=MESH
        )

    locals_ = [
        pltpu.make_async_copy(lat_hbm, win.at[2, c], local_sem.at[0]),
        pltpu.make_async_copy(qn_hbm, qn, local_sem.at[1]),
        pltpu.make_async_copy(qr_hbm, qr, local_sem.at[2]),
    ]

    def own(k, m):
        return pltpu.make_async_copy(
            weights[m].at[:, chunk(k)], wts.at[k, m, z, x, c], local_sem.at[3 + m * steps + k]
        )

    barrier = pltpu.get_barrier_semaphore()
    offsets = (1, 2, 4, 8, n - 4, n - 2, n - 1)
    for d in offsets:
        pl.semaphore_signal(barrier, inc=1, device_id=at_ctx(lax.rem(place + d, n)), device_id_type=MESH)
    pl.semaphore_signal(barrier, inc=1, device_id=y_peer, device_id_type=MESH)
    for copy in locals_:
        copy.start()

    @pl.loop(0, steps)
    def _(k):
        own(k, 0).start()
        own(k, 1).start()

    pl.semaphore_wait(barrier, len(offsets) + 1)

    def z_copy(k, d, m):
        return remote(
            weights[m].at[mine, chunk(k)], wts.at[k, m, z, x, c, mine], z_send.at[k, d - 1, m], z_recv.at[k, d - 1, m], z_peer(d)
        )

    def z_arrival(k, d, m):
        slot = wts.at[k, m, plane(4 - d), x, c, mine]
        return remote(slot, slot, z_send.at[k, d - 1, m], z_recv.at[k, d - 1, m], z_peer(d))

    def x_own(k, m):
        return remote(
            weights[m].at[:, chunk(k)], wts.at[k, m, z, x, c], x_send.at[k, 3 + m], x_recv.at[k, 3 + m], x_peer
        )

    def x_own_arrival(k, m):
        slot = wts.at[k, m, z, 1 - x, c]
        return remote(slot, slot, x_send.at[k, 3 + m], x_recv.at[k, 3 + m], x_peer)

    def x_copy(k, d):
        slot = wts.at[k, :, plane(d), x, c, mine]
        return remote(slot, slot, x_send.at[k, d - 1], x_recv.at[k, d - 1], x_peer)

    def x_arrival(k, d):
        slot = wts.at[k, :, plane(d), 1 - x, c, mine]
        return remote(slot, slot, x_send.at[k, d - 1], x_recv.at[k, d - 1], x_peer)

    def x_relay(k):
        slot = wts.at[k, 1, plane(3), x, c, theirs]
        return remote(slot, slot, x_send.at[k, 5], x_recv.at[k, 5], x_peer)

    def x_relay_arrival(k):
        slot = wts.at[k, 1, plane(3), 1 - x, c, theirs]
        return remote(slot, slot, x_send.at[k, 5], x_recv.at[k, 5], x_peer)

    def y_copy(k, d):
        slot = wts.at[k, :, plane(d), x, c, mine]
        return remote(slot, slot, y_send.at[k, d - 1], y_recv.at[k, d - 1], y_peer)

    def y_arrival(k, d):
        slot = wts.at[k, :, plane(d), x, c, theirs]
        return remote(slot, slot, y_send.at[k, d - 1], y_recv.at[k, d - 1], y_peer)

    def y_relay(k, d):
        slot = wts.at[k, :, plane(d), 1 - x, c, mine] if d < 3 else wts.at[k, 0, plane(d), 1 - x, c, mine]
        return remote(slot, slot, y_send.at[k, d + 2], y_recv.at[k, d + 2], y_peer)

    def y_relay_arrival(k, d):
        slot = wts.at[k, :, plane(d), 1 - x, c, theirs] if d < 3 else wts.at[k, 0, plane(d), 1 - x, c, theirs]
        return remote(slot, slot, y_send.at[k, d + 2], y_recv.at[k, d + 2], y_peer)

    def c_copy(k):
        slot = wts.at[k, :, :, :, c]
        return remote(slot, slot, c_send.at[k], c_recv.at[k], c_peer)

    def c_arrival(k):
        slot = wts.at[k, :, :, :, 1 - c]
        return remote(slot, slot, c_send.at[k], c_recv.at[k], c_peer)

    def lat_copy(d):
        slot = win.at[2 - d, c]
        return remote(lat_hbm, slot, lat_send.at[d], lat_recv.at[d], at_ctx(lax.rem(place + 2 * d, n)))

    def lat_swap():
        slot = win.at[:, c]
        return remote(slot, slot, lat_send.at[0], lat_recv.at[0], c_peer)

    def lat_swap_arrival():
        slot = win.at[:, 1 - c]
        return remote(slot, slot, lat_send.at[0], lat_recv.at[0], c_peer)

    def start_z(k):
        for d in (1, 3, 2):
            for m in range(2):
                z_copy(k, d, m).start()

    def start_x_own(k):
        for m in range(2):
            x_own(k, m).start()

    @pl.loop(0, Z_AHEAD)
    def _(k):
        start_z(k)

    @pl.loop(0, X_AHEAD)
    def _(k):
        start_x_own(k)

    for d in range(1, 3):
        lat_copy(d).start()

    q_pos = place * rows + lax.broadcasted_iota(jnp.int32, (rows, SPREAD * rows), 0)
    k_pos = (place - (SPREAD - 1)) * rows + lax.broadcasted_iota(jnp.int32, (rows, SPREAD * rows), 1)
    low = jnp.zeros_like(q_pos)
    start = jnp.int32(0)
    for e in range(lens.shape[0]):
        low = jnp.where(q_pos >= start, start, low)
        start = start + lens[e]
    bias[...] = jnp.where((k_pos <= q_pos) & (k_pos >= low), jnp.float32(0.0), jnp.float32(-1e30))

    for copy in locals_:
        copy.wait()

    @pl.loop(0, steps)
    def _(k):
        own(k, 0).wait()
        own(k, 1).wait()

    scale = math.log2(math.e) / math.sqrt(DN + DR)
    nt = (((1,), (1,)), ((), ()))
    lane = lax.broadcasted_iota(jnp.int32, (1, 2 * DR), 1)
    sides = [
        (lane < DR).astype(jnp.float32).astype(jnp.bfloat16),
        (lane >= DR).astype(jnp.float32).astype(jnp.bfloat16),
    ]

    def attend_chunk(k):
        for pair in range(HG // 2):
            both = qr[:, pl.ds(pl.multiple_of((k * (HG // 2) + pair) * 2 * DR, 2 * DR), 2 * DR)]
            for side in range(2):
                i = pair * 2 + side
                q = qn[:, pl.ds(pl.multiple_of(k * cols + i * DN, DN), DN)]
                w = wts[k, 0, :, :, :, :, i * DN : (i + 1) * DN].reshape(LAT, DN)
                a = lax.dot_general(q, w, nt, preferred_element_type=jnp.float32)
                lhs[i * rows : (i + 1) * rows, :LAT] = a.astype(jnp.bfloat16)
                lhs[i * rows : (i + 1) * rows, LAT:] = both * sides[side]
        for pair in range(HG // 2):
            part = lhs[pair * 2 * rows : (pair + 1) * 2 * rows, :]
            s = jnp.dot(part, keys[...], preferred_element_type=jnp.float32)
            s = s.reshape(2, rows, SPREAD * rows) * scale + bias[...][None]
            s = s.reshape(2 * rows, SPREAD * rows)
            p = jnp.exp2(s - jnp.max(s, axis=-1, keepdims=True))
            total = jnp.sum(p, axis=-1, keepdims=True)
            mixed = lax.dot_general(p.astype(jnp.bfloat16), keys[:LAT, :], nt, preferred_element_type=jnp.float32)
            mixed = (mixed * (1.0 / total)).astype(jnp.bfloat16)
            for side in range(2):
                i = pair * 2 + side
                w = wts[k, 1, :, :, :, :, i * DV : (i + 1) * DV].reshape(LAT, DV)
                o = jnp.dot(mixed[side * rows : (side + 1) * rows], w, preferred_element_type=jnp.float32)
                out[:, pl.ds(pl.multiple_of(k * cols + i * DV, DV), DV)] = o.astype(out.dtype)

    def finish(k):
        for d in range(1, 4):
            for m in range(2):
                z_copy(k, d, m).wait_send()
            x_copy(k, d).wait_send()
            y_copy(k, d).wait_send()
            y_relay(k, d).wait_send()
        for m in range(2):
            x_own(k, m).wait_send()
        x_relay(k).wait_send()
        c_copy(k).wait_send()

    @pl.loop(0, steps + 3)
    def _(s):
        @pl.when(s < steps)
        def _():
            for d in (1, 3, 2):
                for m in range(2):
                    z_arrival(s, 4 - d, m).wait_recv()
                x_copy(s, d).start()
                y_copy(s, d).start()

        @pl.when(s + X_AHEAD < steps)
        def _():
            start_x_own(s + X_AHEAD)

        @pl.when(s + Z_AHEAD < steps)
        def _():
            start_z(s + Z_AHEAD)

        @pl.when((s >= 1) & (s <= steps))
        def _():
            k = s - 1
            for d in range(1, 4):
                x_arrival(k, d).wait_recv()
                y_relay(k, d).start()
            for d in range(1, 4):
                y_arrival(k, d).wait_recv()
            x_relay(k).start()

        @pl.when((s >= 2) & (s <= steps + 1))
        def _():
            k = s - 2
            for m in range(2):
                x_own_arrival(k, m).wait_recv()
            x_relay_arrival(k).wait_recv()
            for d in range(1, 4):
                y_relay_arrival(k, d).wait_recv()
            c_copy(k).start()

        @pl.when(s == 2)
        def _():
            for d in range(1, 3):
                lat_copy(d).wait_recv()
            lat_swap().start()

        @pl.when(s == 3)
        def _():
            lat_swap_arrival().wait_recv()
            for b in range(SPREAD):
                span = slice(b * rows, (b + 1) * rows)
                block = win[(b + c) // 2, (b + c) % 2]
                keys[: LAT + DR, span] = block
                keys[LAT + DR :, span] = block[LAT:]

        @pl.when(s >= 4)
        def _():
            finish(s - 4)

        @pl.when(s >= 3)
        def _():
            k = s - 3
            c_arrival(k).wait_recv()
            attend_chunk(k)

    for d in range(1, 3):
        lat_copy(d).wait_send()
    lat_swap().wait_send()

    finish(steps - 1)


def kernel_shards(q_nope, q_rope, latent, w_uk, w_uv, doc_lengths):
    rows = q_nope.shape[0]
    steps = HEADS // HG
    window = SPREAD * rows
    anywhere = pl.BlockSpec(memory_space=pltpu.HBM)
    dma = pltpu.SemaphoreType.DMA
    return pl.pallas_call(
        window_kernel,
        out_shape=jax.ShapeDtypeStruct((rows, HEADS * DV), jnp.bfloat16),
        in_specs=[anywhere] * 5 + [pl.BlockSpec(memory_space=pltpu.SMEM)],
        out_specs=pl.BlockSpec(memory_space=pltpu.VMEM),
        scratch_shapes=[
            pltpu.VMEM(q_nope.shape, jnp.bfloat16),
            pltpu.VMEM(q_rope.shape, jnp.bfloat16),
            pltpu.VMEM((3, 2, LAT + DR, rows), jnp.bfloat16),
            pltpu.VMEM((LAT + 2 * DR, window), jnp.bfloat16),
            pltpu.VMEM((rows, window), jnp.float32),
            pltpu.VMEM((HG * rows, LAT + 2 * DR), jnp.bfloat16),
            pltpu.VMEM((steps, 2, 4, 2, 2, w_uk.shape[0], HG * DN), jnp.bfloat16),
            dma((3 + 2 * steps,)),
            dma((3,)),
            dma((3,)),
            dma((steps, 3, 2)),
            dma((steps, 3, 2)),
            dma((steps, 6)),
            dma((steps, 6)),
            dma((steps, 6)),
            dma((steps, 6)),
            dma((steps,)),
            dma((steps,)),
        ],
        compiler_params=pltpu.CompilerParams(
            collective_id=0, has_side_effects=True, vmem_limit_bytes=56 * 1024 * 1024
        ),
    )(q_nope, q_rope, latent.T, w_uk, w_uv, doc_lengths)


def solution(mesh):
    placed = (
        P(("groups", "ctx"), None),
        P(("groups", "ctx"), None),
        P(("groups", "ctx"), None),
        P("ctx", None),
        P("ctx", None),
        P("groups"),
    )
    small = mesh.shape["ctx"] == 16 and mesh.shape["groups"] == 2
    return jax.shard_map(
        kernel_shards if small else shards,
        mesh=mesh,
        in_specs=placed,
        out_specs=P(("groups", "ctx"), None),
        check_vma=False,
    )
```

```python
import math

import jax
import jax.numpy as jnp
from jax import lax
from jax.experimental import pallas as pl
from jax.experimental.pallas import tpu as pltpu
from jax.sharding import PartitionSpec as P

HEADS = 64
DN = 128
DV = 128
DR = 64
LAT = 512
SPAN = 4
MESH = pl.DeviceIdType.MESH
Z_AHEAD = 2
X_AHEAD = 1


def from_behind(block, axis, distance):
    devices = range(lax.axis_size(axis))
    route = [(i - distance, i) for i in devices if i - distance in devices]
    return lax.ppermute(block, axis, route)


def doc_index(starts, positions):
    return jnp.sum((starts[None, :] <= positions[:, None]).astype(jnp.int32), axis=1) - 1


def allowed_pairs(starts, key_start, key_count, q_pos, q_doc):
    k_pos = key_start + jnp.arange(key_count, dtype=jnp.int32)
    k_doc = doc_index(starts, k_pos)
    return (q_doc[:, None] == k_doc[None, :]) & (k_pos[None, :] <= q_pos[:, None])


def attend(state, keys, allowed, absorbed, rope_q, scale):
    top, total, summed = state
    scores = jnp.einsum("thj,kj->thk", absorbed, keys[:, :LAT], preferred_element_type=jnp.float32)
    scores = scores + jnp.einsum(
        "thr,kr->thk", rope_q, keys[:, LAT:], preferred_element_type=jnp.float32
    )
    scores = scores * scale
    mask = allowed[:, None, :]
    fresh = jnp.maximum(top, jnp.max(jnp.where(mask, scores, jnp.float32(-1e30)), axis=-1))
    weights = jnp.where(mask, jnp.exp(scores - fresh[..., None]), jnp.float32(0.0))
    factor = jnp.exp(top - fresh)
    total = total * factor + jnp.sum(weights, axis=-1)
    summed = summed * factor[..., None] + jnp.einsum(
        "thk,kj->thj",
        weights.astype(jnp.bfloat16),
        keys[:, :LAT],
        preferred_element_type=jnp.float32,
    )
    return (fresh, total, summed)


def shards(q_nope, q_rope, latent, w_uk, w_uv, doc_lengths):
    rows_here = q_nope.shape[0]
    scale = 1.0 / math.sqrt(DN + DR)
    place = lax.axis_index("ctx")
    queries = q_nope.reshape(rows_here, HEADS, DN)
    rope_q = q_rope.reshape(rows_here, HEADS, DR)
    piece = lax.all_gather(w_uk, "ctx", axis=0, tiled=True)
    weights = piece.reshape(piece.shape[0], HEADS, DN)
    absorbed = jnp.einsum(
        "thd,jhd->thj", queries, weights, preferred_element_type=jnp.float32
    ).astype(jnp.bfloat16)
    starts = jnp.cumsum(doc_lengths) - doc_lengths
    q_pos = place * rows_here + jnp.arange(rows_here, dtype=jnp.int32)
    q_doc = doc_index(starts, q_pos)
    state = (
        jnp.full((rows_here, HEADS), -1e30, jnp.float32),
        jnp.zeros((rows_here, HEADS), jnp.float32),
        jnp.zeros((rows_here, HEADS, LAT), jnp.float32),
    )

    def take_block(carry, keys, key_start):
        allowed = allowed_pairs(starts, key_start, keys.shape[0], q_pos, q_doc)
        return lax.cond(
            jnp.any(allowed),
            lambda value: attend(value, keys, allowed, absorbed, rope_q, scale),
            lambda value: value,
            carry,
        )

    state = take_block(state, latent, place * rows_here)
    moving = latent
    for back in range(1, SPAN + 1):
        moving = from_behind(moving, "ctx", 1)
        state = take_block(state, moving, (place - back) * rows_here)
    top, total, summed = state
    mixed = (summed / total[..., None]).astype(jnp.bfloat16)
    piece = lax.all_gather(w_uv, "ctx", axis=0, tiled=True)
    rows = piece.shape[0]
    weights = piece.reshape(rows, HEADS, DV)
    term = jnp.einsum("thj,jhd->thd", mixed, weights, preferred_element_type=jnp.float32)
    result = term.reshape(rows_here, HEADS * DV)
    return result.astype(jnp.bfloat16)


HG = 4
SPREAD = 5


def window_kernel(
    qn_hbm, qr_hbm, lat_hbm, uk_hbm, uv_hbm, lens, out,
    qn, qr, win, keys, bias, lhs, wts,
    local_sem, lat_send, lat_recv, z_send, z_recv, x_send, x_recv, y_send, y_recv, c_send, c_recv,
):
    rows = qn_hbm.shape[0]
    steps = HEADS // HG
    cols = HG * DN
    n = lax.axis_size("ctx")
    group = lax.axis_index("groups")
    place = lax.axis_index("ctx")
    z = place // 4
    x = (place // 2) % 2
    c = place % 2
    half = uk_hbm.shape[0] // 2
    mine = pl.ds(pl.multiple_of(group * half, half), half)
    theirs = pl.ds(pl.multiple_of((1 - group) * half, half), half)
    weights = (uk_hbm, uv_hbm)

    def at_ctx(i):
        return (group, i)

    x_peer = at_ctx((z * 2 + (1 - x)) * 2 + c)
    c_peer = at_ctx((z * 2 + x) * 2 + (1 - c))
    y_peer = (1 - group, place)

    def plane(d):
        return lax.rem(z + d, 4)

    def z_peer(d):
        return at_ctx((plane(d) * 2 + x) * 2 + c)

    def chunk(k):
        return pl.ds(pl.multiple_of(k * cols, cols), cols)

    def remote(src, dst, send, recv, peer):
        return pltpu.make_async_remote_copy(
            src_ref=src, dst_ref=dst, send_sem=send, recv_sem=recv, device_id=peer, device_id_type=MESH
        )

    locals_ = [
        pltpu.make_async_copy(lat_hbm, win.at[2, c], local_sem.at[0]),
        pltpu.make_async_copy(qn_hbm, qn, local_sem.at[1]),
        pltpu.make_async_copy(qr_hbm, qr, local_sem.at[2]),
    ]

    def own(k, m):
        return pltpu.make_async_copy(
            weights[m].at[:, chunk(k)], wts.at[k, m, z, x, c], local_sem.at[3 + m * steps + k]
        )

    barrier = pltpu.get_barrier_semaphore()
    offsets = (1, 2, 4, 8, n - 4, n - 2, n - 1)
    for d in offsets:
        pl.semaphore_signal(barrier, inc=1, device_id=at_ctx(lax.rem(place + d, n)), device_id_type=MESH)
    pl.semaphore_signal(barrier, inc=1, device_id=y_peer, device_id_type=MESH)
    for copy in locals_:
        copy.start()

    @pl.loop(0, steps)
    def _(k):
        own(k, 0).start()
        own(k, 1).start()

    pl.semaphore_wait(barrier, len(offsets) + 1)

    def z_copy(k, d, m):
        return remote(
            weights[m].at[mine, chunk(k)], wts.at[k, m, z, x, c, mine], z_send.at[k, d - 1, m], z_recv.at[k, d - 1, m], z_peer(d)
        )

    def z_arrival(k, d, m):
        slot = wts.at[k, m, plane(4 - d), x, c, mine]
        return remote(slot, slot, z_send.at[k, d - 1, m], z_recv.at[k, d - 1, m], z_peer(d))

    def x_own(k, m):
        return remote(
            weights[m].at[:, chunk(k)], wts.at[k, m, z, x, c], x_send.at[k, 3 + m], x_recv.at[k, 3 + m], x_peer
        )

    def x_own_arrival(k, m):
        slot = wts.at[k, m, z, 1 - x, c]
        return remote(slot, slot, x_send.at[k, 3 + m], x_recv.at[k, 3 + m], x_peer)

    def x_copy(k, d):
        slot = wts.at[k, :, plane(d), x, c, mine]
        return remote(slot, slot, x_send.at[k, d - 1], x_recv.at[k, d - 1], x_peer)

    def x_arrival(k, d):
        slot = wts.at[k, :, plane(d), 1 - x, c, mine]
        return remote(slot, slot, x_send.at[k, d - 1], x_recv.at[k, d - 1], x_peer)

    def x_relay(k):
        slot = wts.at[k, 1, plane(3), x, c, theirs]
        return remote(slot, slot, x_send.at[k, 5], x_recv.at[k, 5], x_peer)

    def x_relay_arrival(k):
        slot = wts.at[k, 1, plane(3), 1 - x, c, theirs]
        return remote(slot, slot, x_send.at[k, 5], x_recv.at[k, 5], x_peer)

    def y_copy(k, d):
        slot = wts.at[k, :, plane(d), x, c, mine]
        return remote(slot, slot, y_send.at[k, d - 1], y_recv.at[k, d - 1], y_peer)

    def y_arrival(k, d):
        slot = wts.at[k, :, plane(d), x, c, theirs]
        return remote(slot, slot, y_send.at[k, d - 1], y_recv.at[k, d - 1], y_peer)

    def y_relay(k, d):
        slot = wts.at[k, :, plane(d), 1 - x, c, mine] if d < 3 else wts.at[k, 0, plane(d), 1 - x, c, mine]
        return remote(slot, slot, y_send.at[k, d + 2], y_recv.at[k, d + 2], y_peer)

    def y_relay_arrival(k, d):
        slot = wts.at[k, :, plane(d), 1 - x, c, theirs] if d < 3 else wts.at[k, 0, plane(d), 1 - x, c, theirs]
        return remote(slot, slot, y_send.at[k, d + 2], y_recv.at[k, d + 2], y_peer)

    def c_copy(k):
        slot = wts.at[k, :, :, :, c]
        return remote(slot, slot, c_send.at[k], c_recv.at[k], c_peer)

    def c_arrival(k):
        slot = wts.at[k, :, :, :, 1 - c]
        return remote(slot, slot, c_send.at[k], c_recv.at[k], c_peer)

    def lat_copy(d):
        slot = win.at[2 - d, c]
        return remote(lat_hbm, slot, lat_send.at[d], lat_recv.at[d], at_ctx(lax.rem(place + 2 * d, n)))

    def lat_swap():
        slot = win.at[:, c]
        return remote(slot, slot, lat_send.at[0], lat_recv.at[0], c_peer)

    def lat_swap_arrival():
        slot = win.at[:, 1 - c]
        return remote(slot, slot, lat_send.at[0], lat_recv.at[0], c_peer)

    def start_z(k):
        for d in (2, 1, 3):
            for m in range(2):
                z_copy(k, d, m).start()

    def start_x_own(k):
        for m in range(2):
            x_own(k, m).start()

    for d in range(1, 3):
        lat_copy(d).start()

    @pl.loop(0, Z_AHEAD)
    def _(k):
        start_z(k)

    @pl.loop(0, X_AHEAD)
    def _(k):
        start_x_own(k)

    q_pos = place * rows + lax.broadcasted_iota(jnp.int32, (rows, SPREAD * rows), 0)
    k_pos = (place - (SPREAD - 1)) * rows + lax.broadcasted_iota(jnp.int32, (rows, SPREAD * rows), 1)
    low = jnp.zeros_like(q_pos)
    start = jnp.int32(0)
    for e in range(lens.shape[0]):
        low = jnp.where(q_pos >= start, start, low)
        start = start + lens[e]
    bias[...] = jnp.where((k_pos <= q_pos) & (k_pos >= low), jnp.float32(0.0), jnp.float32(-1e30))

    for copy in locals_:
        copy.wait()

    @pl.loop(0, steps)
    def _(k):
        own(k, 0).wait()
        own(k, 1).wait()

    scale = math.log2(math.e) / math.sqrt(DN + DR)
    nt = (((1,), (1,)), ((), ()))
    lane = lax.broadcasted_iota(jnp.int32, (1, 2 * DR), 1)
    sides = [
        (lane < DR).astype(jnp.float32).astype(jnp.bfloat16),
        (lane >= DR).astype(jnp.float32).astype(jnp.bfloat16),
    ]

    def attend_chunk(k):
        for pair in range(HG // 2):
            both = qr[:, pl.ds(pl.multiple_of((k * (HG // 2) + pair) * 2 * DR, 2 * DR), 2 * DR)]
            for side in range(2):
                i = pair * 2 + side
                q = qn[:, pl.ds(pl.multiple_of(k * cols + i * DN, DN), DN)]
                w = wts[k, 0, :, :, :, :, i * DN : (i + 1) * DN].reshape(LAT, DN)
                a = lax.dot_general(q, w, nt, preferred_element_type=jnp.float32)
                lhs[i * rows : (i + 1) * rows, :LAT] = a.astype(jnp.bfloat16)
                lhs[i * rows : (i + 1) * rows, LAT:] = both * sides[side]
        for pair in range(HG // 2):
            part = lhs[pair * 2 * rows : (pair + 1) * 2 * rows, :]
            s = jnp.dot(part, keys[...], preferred_element_type=jnp.float32)
            s = s.reshape(2, rows, SPREAD * rows) * scale + bias[...][None]
            s = s.reshape(2 * rows, SPREAD * rows)
            p = jnp.exp2(s - jnp.max(s, axis=-1, keepdims=True))
            total = jnp.sum(p, axis=-1, keepdims=True)
            mixed = lax.dot_general(p.astype(jnp.bfloat16), keys[:LAT, :], nt, preferred_element_type=jnp.float32)
            mixed = (mixed * (1.0 / total)).astype(jnp.bfloat16)
            for side in range(2):
                i = pair * 2 + side
                w = wts[k, 1, :, :, :, :, i * DV : (i + 1) * DV].reshape(LAT, DV)
                o = jnp.dot(mixed[side * rows : (side + 1) * rows], w, preferred_element_type=jnp.float32)
                out[:, pl.ds(pl.multiple_of(k * cols + i * DV, DV), DV)] = o.astype(out.dtype)

    def finish(k):
        for d in range(1, 4):
            for m in range(2):
                z_copy(k, d, m).wait_send()
            x_copy(k, d).wait_send()
            y_copy(k, d).wait_send()
            y_relay(k, d).wait_send()
        for m in range(2):
            x_own(k, m).wait_send()
        x_relay(k).wait_send()
        c_copy(k).wait_send()

    @pl.loop(0, steps + 3)
    def _(s):
        @pl.when(s < steps)
        def _():
            for d in (1, 3, 2):
                for m in range(2):
                    z_arrival(s, 4 - d, m).wait_recv()
                x_copy(s, d).start()
                y_copy(s, d).start()

        @pl.when(s + X_AHEAD < steps)
        def _():
            start_x_own(s + X_AHEAD)

        @pl.when(s + Z_AHEAD < steps)
        def _():
            start_z(s + Z_AHEAD)

        @pl.when((s >= 1) & (s <= steps))
        def _():
            k = s - 1
            for d in range(1, 4):
                x_arrival(k, d).wait_recv()
                y_relay(k, d).start()
            for d in range(1, 4):
                y_arrival(k, d).wait_recv()
            x_relay(k).start()

        @pl.when((s >= 2) & (s <= steps + 1))
        def _():
            k = s - 2
            for m in range(2):
                x_own_arrival(k, m).wait_recv()
            x_relay_arrival(k).wait_recv()
            for d in range(1, 4):
                y_relay_arrival(k, d).wait_recv()
            c_copy(k).start()

        @pl.when(s == 2)
        def _():
            for d in range(1, 3):
                lat_copy(d).wait_recv()
            lat_swap().start()

        @pl.when(s == 3)
        def _():
            lat_swap_arrival().wait_recv()
            for b in range(SPREAD):
                span = slice(b * rows, (b + 1) * rows)
                block = win[(b + c) // 2, (b + c) % 2]
                keys[: LAT + DR, span] = block
                keys[LAT + DR :, span] = block[LAT:]

        @pl.when(s >= 4)
        def _():
            finish(s - 4)

        @pl.when(s >= 3)
        def _():
            k = s - 3
            c_arrival(k).wait_recv()
            attend_chunk(k)

    for d in range(1, 3):
        lat_copy(d).wait_send()
    lat_swap().wait_send()

    finish(steps - 1)


def kernel_shards(q_nope, q_rope, latent, w_uk, w_uv, doc_lengths):
    rows = q_nope.shape[0]
    steps = HEADS // HG
    window = SPREAD * rows
    anywhere = pl.BlockSpec(memory_space=pltpu.HBM)
    dma = pltpu.SemaphoreType.DMA
    return pl.pallas_call(
        window_kernel,
        out_shape=jax.ShapeDtypeStruct((rows, HEADS * DV), jnp.bfloat16),
        in_specs=[anywhere] * 5 + [pl.BlockSpec(memory_space=pltpu.SMEM)],
        out_specs=pl.BlockSpec(memory_space=pltpu.VMEM),
        scratch_shapes=[
            pltpu.VMEM(q_nope.shape, jnp.bfloat16),
            pltpu.VMEM(q_rope.shape, jnp.bfloat16),
            pltpu.VMEM((3, 2, LAT + DR, rows), jnp.bfloat16),
            pltpu.VMEM((LAT + 2 * DR, window), jnp.bfloat16),
            pltpu.VMEM((rows, window), jnp.float32),
            pltpu.VMEM((HG * rows, LAT + 2 * DR), jnp.bfloat16),
            pltpu.VMEM((steps, 2, 4, 2, 2, w_uk.shape[0], HG * DN), jnp.bfloat16),
            dma((3 + 2 * steps,)),
            dma((3,)),
            dma((3,)),
            dma((steps, 3, 2)),
            dma((steps, 3, 2)),
            dma((steps, 6)),
            dma((steps, 6)),
            dma((steps, 6)),
            dma((steps, 6)),
            dma((steps,)),
            dma((steps,)),
        ],
        compiler_params=pltpu.CompilerParams(
            collective_id=0, has_side_effects=True, vmem_limit_bytes=56 * 1024 * 1024
        ),
    )(q_nope, q_rope, latent.T, w_uk, w_uv, doc_lengths)


def solution(mesh):
    placed = (
        P(("groups", "ctx"), None),
        P(("groups", "ctx"), None),
        P(("groups", "ctx"), None),
        P("ctx", None),
        P("ctx", None),
        P("groups"),
    )
    small = mesh.shape["ctx"] == 16 and mesh.shape["groups"] == 2
    return jax.shard_map(
        kernel_shards if small else shards,
        mesh=mesh,
        in_specs=placed,
        out_specs=P(("groups", "ctx"), None),
        check_vma=False,
    )
```
